32 devices in a mesh: clip: 4 (over z), row: 4 (over y, core), ch: 2 (over x).
Axes of the slice: x: 2, y: 2, z: 4, core: 2. Of those that a mesh axis runs over, the one named last changes fastest.
Arguments:
- features: bfloat16 [4, 4, 32, 512, 256], P('clip', None, 'row', None, 'ch'), may hold values from -6 to 6
- weight: bfloat16 [3, 3, 3, 3, 256], P(None, None, None, None, 'ch'), may hold values from -0.078125 to 0.078125
- target: bfloat16 [4, 3, 2, 32, 512], P('clip', None, None, 'row'), may hold values from -6 to 6
Outputs:
- grad_features: bfloat16 [4, 4, 32, 512, 256], P('clip', None, 'row', None, 'ch')
- grad_weight: float32 [3, 3, 3, 3, 256], P(None, None, None, None, 'ch')
- focal_loss: float32 [4], P('clip')
The draws below stay inside these ranges and needn't reach their ends.
All inputs are finite; a program needn't handle non-finite values.
Results may differ from the reference program's by a relative error of at most 0.0049.
Values may be sent and summed in bfloat16 or wider, within the bound.
A program may use at most 64 MiB of HBM per device.

```python
import math
from functools import partial
import jax
import jax.numpy as jnp
from jax import lax

CHAN = 256
COLS = 512
FRAMES = 2
FRAMES_IN = 4
HEIGHT = 32
CLIPS = 4


def levels(key, extent, shards, least, largest):
    def one(axis_at, blocks):
        draws = jax.random.uniform(jax.random.fold_in(jax.random.fold_in(key, 6), axis_at), (blocks,), jnp.float32, least / len(shards), largest / len(shards))
        return jnp.repeat(jnp.exp(draws), extent[axis_at] // blocks).reshape((-1,) + (1,) * (len(extent) - axis_at - 1))

    gain = one(*shards[0])
    for cut in shards[1:]:
        gain = gain * one(*cut)
    return gain


def bell_draw(stream_key, extent, width, bound, cuts=(), kind=jnp.bfloat16):
    entries = width * jax.random.normal(stream_key, extent, jnp.float32)
    if cuts:
        entries = entries * levels(stream_key, extent, cuts, -0.22, 0.18)
    return jnp.clip(entries, -bound, bound).astype(kind)


def setup_inputs(seed: int = 0) -> dict:
    arg_keys = jax.random.split(jax.random.key(seed), 4)
    return {
        "features": bell_draw(arg_keys[0], (CLIPS, FRAMES_IN, HEIGHT, COLS, CHAN), 1.0, 6.0, ((0, 4), (2, 4), (4, 2))),
        "weight": bell_draw(arg_keys[1], (3, 3, 3, 3, CHAN), (27 * CHAN) ** -0.5, 0.078125, ((4, 2),)),
        "target": bell_draw(arg_keys[2], (CLIPS, 3, FRAMES, HEIGHT, COLS), 1.0, 6.0, ((0, 4), (3, 4))),
    }


def column_table(columns):
    column_ids = jnp.arange(columns, dtype=jnp.int32)
    frequency_ids = jnp.arange(columns // 2, dtype=jnp.int32)
    phases = 2.0 * math.pi / columns * (column_ids[:, None] * frequency_ids[None, :] % columns).astype(jnp.float32)
    factor = 1.0 / math.sqrt(columns)
    return factor * jnp.stack([jnp.cos(phases), -jnp.sin(phases)], axis=1)

def row_table(height):
    row_ids = jnp.arange(height, dtype=jnp.int32)
    phases = 2.0 * math.pi / height * (row_ids[:, None] * row_ids[None, :] % height).astype(jnp.float32)
    factor = 1.0 / math.sqrt(height)
    cosine = factor * jnp.cos(phases)
    sine_part = factor * jnp.sin(phases)
    return jnp.stack([jnp.stack([cosine, -sine_part], axis=1), jnp.stack([sine_part, cosine], axis=1)], axis=0)

def tap_total(padded, frames_out, count, columns):
    running = 0.0
    for time_tap in range(3):
        for row_tap in range(3):
            for column_tap in range(3):
                running = running + padded[time_tap, row_tap, column_tap, :, time_tap:time_tap + frames_out, row_tap:row_tap + count, column_tap:column_tap + columns]
    return running

def one_clip(kernel, column_basis, row_basis, inputs):
    clip_in, clip_target = inputs
    frames_in, height, columns, channels = clip_in.shape
    frames_out = frames_in - 2
    source = clip_in.astype(jnp.float32)
    tap_terms = jnp.einsum('kc,thwc->kthw', kernel, source, precision=lax.Precision.HIGHEST)
    tap_terms = tap_terms.reshape(3, 3, 3, 3, frames_in, height, columns)
    tap_terms = jnp.pad(tap_terms, ((0, 0),) * 5 + ((1, 1), (1, 1)))
    output = tap_total(tap_terms, frames_out, height, columns)
    residual = output - clip_target.astype(jnp.float32)
    spectra = jnp.einsum('ofhw,wpk->ofpkh', residual, column_basis, precision=lax.Precision.HIGHEST)
    spectrum = jnp.einsum('ofpkh,phqg->ofqkg', spectra, row_basis, precision=lax.Precision.HIGHEST)
    spectral_power = spectrum[:, :, 0] ** 2 + spectrum[:, :, 1] ** 2
    power_peak = lax.optimization_barrier(jnp.max(spectral_power, axis=(2, 3)))
    focal_weight = spectral_power / (power_peak[:, :, None, None] + 1e-05)
    entry_count = frames_out * 3 * height * (columns // 2)
    loss_value = jnp.sum(focal_weight * spectral_power) / entry_count
    upstream = 2.0 * focal_weight[:, :, None] * spectrum
    row_grads = jnp.einsum('ofqkg,phqg->ofpkh', upstream, row_basis, precision=lax.Precision.HIGHEST)
    grad_out = jnp.einsum('ofpkh,wpk->ofhw', row_grads, column_basis, precision=lax.Precision.HIGHEST)
    grad_rounded = grad_out.astype(jnp.bfloat16).astype(jnp.float32)
    padded = jnp.pad(grad_rounded, ((0, 0), (2, 2), (1, 1), (1, 1)))
    tap_list = []
    for time_tap in range(3):
        for row_tap in range(3):
            for column_tap in range(3):
                tap_list.append(padded[:, 2 - time_tap:2 - time_tap + frames_in, 2 - row_tap:2 - row_tap + height, 2 - column_tap:2 - column_tap + columns])
    shifted = jnp.stack(tap_list, axis=0).reshape(81, frames_in, height, columns)
    feature_grads = jnp.einsum('kthw,kc->thwc', shifted, kernel, precision=lax.Precision.HIGHEST).astype(jnp.bfloat16)
    weight_grads = jnp.einsum('kthw,thwc->kc', shifted, source, precision=lax.Precision.HIGHEST)
    return (feature_grads, weight_grads, loss_value)

def reference(features, weight, target):
    channels = weight.shape[-1]
    kernel = weight.astype(jnp.float32).reshape(81, channels)
    height = features.shape[2]
    columns = features.shape[3]
    column_basis = column_table(columns)
    row_basis = row_table(height)
    feature_grads, weight_grads, losses = lax.map(partial(one_clip, kernel, column_basis, row_basis), (features, target))
    grad_weight = lax.optimization_barrier(jnp.sum(weight_grads, axis=0)).reshape(3, 3, 3, 3, channels)
    return (feature_grads, grad_weight, losses)
```

```python
import functools
import math

import jax
import jax.numpy as jnp
import ml_dtypes
import numpy as np
from jax import lax
from jax.experimental import pallas as pl
from jax.experimental.pallas import tpu as pltpu
from jax.sharding import PartitionSpec as P

MESH = pl.DeviceIdType.MESH
BLOCK = 16
F32 = jnp.float32
BF16 = jnp.bfloat16


def split_table(table):
    high = table.astype(ml_dtypes.bfloat16)
    low = (table - high.astype(np.float64)).astype(ml_dtypes.bfloat16)
    return high, low


def column_table(columns):
    phases = np.outer(np.arange(columns), np.arange(columns // 2)) % columns
    phases = 2.0 * math.pi / columns * phases
    return np.concatenate([np.cos(phases), -np.sin(phases)], axis=1) / math.sqrt(columns)


def row_table(height, rows_dev):
    table = np.zeros((2 * height, height // rows_dev * BLOCK))
    ids = np.arange(height)
    for device in range(height // rows_dev):
        for entry in range(rows_dev + 2):
            row = device * rows_dev + rows_dev - entry
            if 0 <= row < height:
                phase = 2.0 * math.pi / height * (ids * row % height)
                table[:height, device * BLOCK + entry] = np.cos(phase)
                table[height:, device * BLOCK + entry] = -np.sin(phase)
    return table / math.sqrt(height)


def halves(x):
    high = x.astype(BF16)
    return high, (x - high.astype(F32)).astype(BF16)


def dot(a, b, dims=((1,), (0,))):
    return lax.dot_general(a, b, (dims, ((), ())), preferred_element_type=F32)


def dot3(a, b, dims=((1,), (0,))):
    return dot(a[0], b[0], dims) + (dot(a[0], b[1], dims) + dot(a[1], b[0], dims))


def shift(x, by):
    columns = x.shape[-1]
    lane = lax.broadcasted_iota(jnp.int32, x.shape, 1)
    if by > 0:
        return jnp.where(lane < by, 0.0, pltpu.roll(x, by, 1))
    return jnp.where(lane >= columns + by, 0.0, pltpu.roll(x, columns + by, 1))


def main_kernel(
    sizes,
    features,
    weight,
    target,
    row_high,
    row_low,
    back_high,
    back_low,
    col_high_any,
    col_low_any,
    shifted_out,
    weight_out,
    grad_weight,
    loss_out,
    held,
    col_high,
    col_low,
    acc,
    weight_acc,
    part,
    arrived,
    grad_send,
    grad_all,
    shifted,
    kernel_acc,
    terms,
    terms_in,
    terms_sum,
    load_sem,
    send_sem,
    recv_sem,
    back_send,
    back_recv,
    terms_send,
    terms_recv,
    sum_send,
    sum_recv,
):
    n_clip, n_row, n_ch, chunk, n_own = sizes
    frames_in, rows_dev, columns, channels = held.shape
    frames_out = frames_in - 2
    planes = 3 * frames_out
    n_group = n_row * n_ch
    n_all = n_clip * n_row
    clip, row, ch = (lax.axis_index(a) for a in ("clip", "row", "ch"))
    me = row * n_ch + ch
    rank = clip * n_row + row
    entries = float(planes * n_row * rows_dev * (columns // 2))

    loads = [
        pltpu.make_async_copy(features.at[0, f], held.at[f], load_sem.at[f])
        for f in range(frames_in)
    ]
    loads.append(pltpu.make_async_copy(col_high_any, col_high, load_sem.at[frames_in]))
    loads.append(pltpu.make_async_copy(col_low_any, col_low, load_sem.at[frames_in + 1]))
    for load in loads:
        load.start()

    barrier = pltpu.get_barrier_semaphore()

    @pl.loop(1, n_group)
    def _(p):
        other = lax.rem(me + p, n_group)
        pl.semaphore_signal(
            barrier,
            inc=1,
            device_id={"row": other // n_ch, "ch": lax.rem(other, n_ch)},
            device_id_type=MESH,
        )

    @pl.loop(n_row, n_all)
    def _(p):
        other = lax.rem(clip * n_row + p, n_all)
        pl.semaphore_signal(
            barrier,
            inc=1,
            device_id={"clip": other // n_row, "row": lax.rem(other, n_row)},
            device_id_type=MESH,
        )

    weight_acc[...] = jnp.zeros_like(weight_acc)
    for dt in range(3):
        for di in range(3):
            for dj in range(3):
                at = (dt * 3 + di) * BLOCK + dj * 3
                weight_acc[at : at + 3, :] = weight[dt, di, dj].astype(F32)
    taps = weight_acc[...].astype(BF16)
    weight_out[...] = taps

    acc[...] = jnp.zeros_like(acc)

    @pl.when(ch == 0)
    def _():
        for t in range(frames_out):
            for o in range(3):
                frame = -target[0, o, t].astype(F32)
                for i in range(rows_dev):
                    acc[t, rows_dev - i, 3 + o, :] = frame[i]

    def exchange(t):
        for o in range(3):
            views = [acc[t, :, dj * 3 + o, :] for dj in range(3)]
            part[t * 3 + o] = views[1] + shift(views[0], 1) + shift(views[2], -1)
            plane = t * 3 + o

            @pl.when(me == plane)
            def _():
                arrived[plane] = part[plane]

            @pl.when(me != plane)
            def _():
                pltpu.make_async_remote_copy(
                    src_ref=part.at[plane],
                    dst_ref=arrived.at[me],
                    send_sem=send_sem.at[plane],
                    recv_sem=recv_sem.at[me],
                    device_id={"row": plane // n_ch, "ch": plane % n_ch},
                    device_id_type=MESH,
                ).start()

    for f in range(frames_in):
        loads[f].wait()
        low, top = max(0, f - frames_out + 1), min(2, f)
        chosen = taps[low * 3 * BLOCK : (top + 1) * 3 * BLOCK]

        @pl.loop(0, rows_dev, unroll=True)
        def _(r):
            made = dot(chosen, held[f, r], ((1,), (1,))).reshape(-1, BLOCK, columns)
            for dt in range(low, top + 1):
                at = (dt - low) * 3
                acc[f - dt, pl.ds(rows_dev - 1 - r, 3)] += made[at : at + 3]

        if f == 2:
            pl.semaphore_wait(barrier, n_group - 1 + n_all - n_row)
        if f >= 2:
            exchange(f - 2)

    loads[frames_in].wait()
    loads[frames_in + 1].wait()

    @pl.when(me < planes)
    def _():
        @pl.loop(0, n_group)
        def _(s):
            @pl.when(s != me)
            def _():
                pltpu.make_async_copy(
                    arrived.at[s], arrived.at[s], recv_sem.at[s]
                ).wait()

        blocks = []
        for r in range(n_row):
            total = arrived[r * n_ch]
            for c in range(1, n_ch):
                total = total + arrived[r * n_ch + c]
            blocks.append(total)
        residual = jnp.concatenate(blocks, axis=0)
        height = n_row * rows_dev
        half = columns // 2
        basis = (col_high[...], col_low[...])
        rows_done = dot3((row_high[...], row_low[...]), halves(residual))
        both = dot3(halves(rows_done), basis)
        real = both[:height, :half] - both[height:, half:]
        imag = both[height:, :half] + both[:height, half:]
        power = real * real + imag * imag
        peak = jnp.max(power, keepdims=True)
        focal = power / (peak + 1e-05)
        loss = jnp.sum(focal * power, keepdims=True) / entries
        up_real = 2.0 * focal * real
        up_imag = 2.0 * focal * imag
        upstream = jnp.concatenate(
            [
                jnp.concatenate([up_real, up_imag], axis=1),
                jnp.concatenate([up_imag, -up_real], axis=1),
            ],
            axis=0,
        )
        columns_done = dot3(halves(upstream), basis, ((1,), (1,)))
        grads = dot3((back_high[...], back_low[...]), halves(columns_done))
        loss_high = loss.astype(BF16).astype(F32)
        loss_mid = (loss - loss_high).astype(BF16).astype(F32)
        loss_low = loss - loss_high - loss_mid
        entry = lax.rem(lax.broadcasted_iota(jnp.int32, grads.shape, 0), BLOCK)
        grads = jnp.where(entry == rows_dev + 2, loss_high, grads)
        grads = jnp.where(entry == rows_dev + 3, loss_mid, grads)
        grads = jnp.where(entry == rows_dev + 4, loss_low, grads)
        grads = grads.astype(BF16)
        for r in range(n_row):
            grad_send[r] = grads[r * BLOCK : (r + 1) * BLOCK]

        @pl.loop(1, n_group)
        def _(p):
            other = lax.rem(me + p, n_group)
            pltpu.make_async_remote_copy(
                src_ref=grad_send.at[other // n_ch],
                dst_ref=grad_all.at[me],
                send_sem=back_send.at[p],
                recv_sem=back_recv.at[me],
                device_id={"row": other // n_ch, "ch": lax.rem(other, n_ch)},
                device_id_type=MESH,
            ).start()

        grad_all[me] = grad_send[row]

    acc[...] = jnp.zeros_like(acc)
    for plane in range(planes):
        @pl.when(me != plane)
        def _():
            pltpu.make_async_copy(
                grad_all.at[plane], grad_all.at[plane], back_recv.at[plane]
            ).wait()

    loss_total = jnp.zeros((1, 128), F32)
    for plane in range(planes):
        t, o = divmod(plane, 3)
        grads = grad_all[plane].astype(F32)
        for part_at in range(3):
            at = rows_dev + 2 + part_at
            loss_total = loss_total + grads[at : at + 1, :128]
        entry = lax.broadcasted_iota(jnp.int32, grads.shape, 0)
        grads = jnp.where(entry < rows_dev + 2, grads, 0.0)
        for dj in range(3):
            moved = grads if dj == 1 else shift(grads, dj - 1)
            acc[t, :, dj * 3 + o, :] = moved
    loss_out[...] = loss_total
    for t in range(frames_out):
        shifted[t] = acc[t].reshape(BLOCK * BLOCK, columns).astype(BF16)
    shifted_out[...] = shifted[...]

    kernel_acc[...] = jnp.zeros_like(kernel_acc)

    for f in range(frames_in):
        low, top = max(0, f - frames_out + 1), min(2, f)
        total = 0.0
        for r in range(rows_dev):
            begin = (rows_dev - 1 - r) * BLOCK
            stack = jnp.concatenate(
                [shifted[f - dt, begin : begin + 3 * BLOCK, :] for dt in range(low, top + 1)],
                axis=0,
            )
            total = total + dot(stack, held[f, r])
        kernel_acc[low * 3 * BLOCK : (top + 1) * 3 * BLOCK, :] += total

    terms[...] = jnp.zeros_like(terms)
    for b in range(9):
        terms[b * 9 : b * 9 + 9, :] = kernel_acc[b * BLOCK : b * BLOCK + 9, :]

    for m in range(n_own):
        @pl.when(rank == m)
        def _():
            terms_in[m] = terms[m * chunk : (m + 1) * chunk, :]

        @pl.when(rank != m)
        def _():
            pltpu.make_async_remote_copy(
                src_ref=terms.at[pl.ds(m * chunk, chunk)],
                dst_ref=terms_in.at[rank],
                send_sem=terms_send.at[m],
                recv_sem=terms_recv.at[rank],
                device_id={"clip": m // n_row, "row": m % n_row},
                device_id_type=MESH,
            ).start()

    @pl.when(rank < n_own)
    def _():
        @pl.loop(0, n_all)
        def _(s):
            @pl.when(s != rank)
            def _():
                pltpu.make_async_copy(
                    terms_in.at[s], terms_in.at[s], terms_recv.at[s]
                ).wait()

        terms_sum[rank] = jnp.sum(terms_in[...], axis=0)

        @pl.loop(1, n_all)
        def _(p):
            other = lax.rem(rank + p, n_all)
            pltpu.make_async_remote_copy(
                src_ref=terms_sum.at[rank],
                dst_ref=terms_sum.at[rank],
                send_sem=sum_send.at[p],
                recv_sem=sum_recv.at[rank],
                device_id={"clip": other // n_row, "row": lax.rem(other, n_row)},
                device_id_type=MESH,
            ).start()

    for m in range(n_own):
        @pl.when(rank != m)
        def _():
            pltpu.make_async_copy(
                terms_sum.at[m], terms_sum.at[m], sum_recv.at[m]
            ).wait()

    for k in range(27):
        dt, di, dj = k // 9, k // 3 % 3, k % 3
        for o in range(3):
            m, at = divmod(k * 3 + o, chunk)
            grad_weight[dt, di, dj, o : o + 1, :] = terms_sum[m, at : at + 1, :]

    for plane in range(planes):
        @pl.when(me != plane)
        def _():
            pltpu.make_async_copy(part.at[plane], part.at[plane], send_sem.at[plane]).wait()

    @pl.when(me < planes)
    def _():
        @pl.loop(1, n_group)
        def _(p):
            pltpu.make_async_copy(grad_send.at[0], grad_send.at[0], back_send.at[p]).wait()

    for m in range(n_own):
        @pl.when(rank != m)
        def _():
            piece = terms.at[pl.ds(m * chunk, chunk)]
            pltpu.make_async_copy(piece, piece, terms_send.at[m]).wait()

    @pl.when(rank < n_own)
    def _():
        @pl.loop(1, n_all)
        def _(p):
            pltpu.make_async_copy(
                terms_sum.at[rank], terms_sum.at[rank], sum_send.at[p]
            ).wait()


def features_kernel(frames_out, shifted, taps, grad):
    rows_dev, columns, channels = grad.shape[2:]
    for f in range(frames_out + 2):
        @pl.when(pl.program_id(0) == f)
        def _():
            low, top = max(0, f - frames_out + 1), min(2, f)
            chosen = taps[low * 3 * BLOCK : (top + 1) * 3 * BLOCK, :]
            for r in range(rows_dev):
                begin = (rows_dev - 1 - r) * BLOCK
                stack = jnp.concatenate(
                    [shifted[f - dt, begin : begin + 3 * BLOCK, :] for dt in range(low, top + 1)],
                    axis=0,
                )
                grad[0, 0, r] = dot(stack, chosen, ((0,), (0,))).astype(BF16)


def shards(features, weight, target):
    _, frames_in, rows_dev, columns, channels = features.shape
    frames_out = frames_in - 2
    planes = 3 * frames_out
    n_clip, n_row, n_ch = (lax.axis_size(a) for a in ("clip", "row", "ch"))
    n_group, n_all = n_row * n_ch, n_clip * n_row
    assert planes <= n_group and rows_dev + 5 <= BLOCK
    height = n_row * rows_dev
    pieces = -(-81 // 8)
    chunk = 8 * -(-pieces // n_all)
    n_own = -(-81 // chunk)
    rows = row_table(height, rows_dev)
    tables = (
        *split_table(rows),
        *split_table(np.ascontiguousarray(rows.T)),
        *split_table(column_table(columns)),
    )
    vmem = pl.BlockSpec(memory_space=pltpu.VMEM)
    anywhere = pl.BlockSpec(memory_space=pl.ANY)
    dma = pltpu.SemaphoreType.DMA
    shifted, taps, grad_weight, loss = pl.pallas_call(
        functools.partial(main_kernel, (n_clip, n_row, n_ch, chunk, n_own)),
        out_shape=(
            jax.ShapeDtypeStruct((frames_out, BLOCK * BLOCK, columns), BF16),
            jax.ShapeDtypeStruct((9 * BLOCK, channels), BF16),
            jax.ShapeDtypeStruct((3, 3, 3, 3, channels), F32),
            jax.ShapeDtypeStruct((1, 128), F32),
        ),
        in_specs=[anywhere] + [vmem] * 6 + [anywhere] * 2,
        out_specs=(vmem,) * 4,
        scratch_shapes=[
            pltpu.VMEM((frames_in, rows_dev, columns, channels), BF16),
            pltpu.VMEM((columns, columns), BF16),
            pltpu.VMEM((columns, columns), BF16),
            pltpu.VMEM((frames_out, BLOCK, BLOCK, columns), F32),
            pltpu.VMEM((9 * BLOCK, channels), F32),
            pltpu.VMEM((planes, BLOCK, columns), F32),
            pltpu.VMEM((n_group, BLOCK, columns), F32),
            pltpu.VMEM((n_row, BLOCK, columns), BF16),
            pltpu.VMEM((planes, BLOCK, columns), BF16),
            pltpu.VMEM((frames_out, BLOCK * BLOCK, columns), BF16),
            pltpu.VMEM((9 * BLOCK, channels), F32),
            pltpu.VMEM((n_own * chunk, channels), F32),
            pltpu.VMEM((n_all, chunk, channels), F32),
            pltpu.VMEM((n_own, chunk, channels), F32),
            dma((frames_in + 2,)),
            dma((planes,)),
            dma((n_group,)),
            dma((n_group,)),
            dma((planes,)),
            dma((n_own,)),
            dma((n_all,)),
            dma((n_all,)),
            dma((n_own,)),
        ],
        compiler_params=pltpu.CompilerParams(
            collective_id=0, has_side_effects=True, vmem_limit_bytes=48 * 1024 * 1024
        ),
        name="main",
    )(features, weight, target, *tables)
    grad_features = pl.pallas_call(
        functools.partial(features_kernel, frames_out),
        grid=(frames_in,),
        out_shape=jax.ShapeDtypeStruct(features.shape, BF16),
        in_specs=[
            pl.BlockSpec(shifted.shape, lambda f: (0, 0, 0)),
            pl.BlockSpec(taps.shape, lambda f: (0, 0)),
        ],
        out_specs=pl.BlockSpec(
            (1, 1, rows_dev, columns, channels), lambda f: (0, f, 0, 0, 0)
        ),
        compiler_params=pltpu.CompilerParams(vmem_limit_bytes=48 * 1024 * 1024),
        name="features",
    )(shifted, taps)
    return (grad_features, grad_weight, loss[0, :1])


def solution(mesh):
    placed = (
        P("clip", None, "row", None, "ch"),
        P(None, None, None, None, "ch"),
        P("clip", None, None, "row", None),
    )
    return jax.shard_map(
        shards,
        mesh=mesh,
        in_specs=placed,
        out_specs=(P("clip", None, "row", None, "ch"), P(None, None, None, None, "ch"), P("clip")),
        check_vma=False,
    )
```

```python
import functools
import math

import jax
import jax.numpy as jnp
import ml_dtypes
import numpy as np
from jax import lax
from jax.experimental import pallas as pl
from jax.experimental.pallas import tpu as pltpu
from jax.sharding import PartitionSpec as P

MESH = pl.DeviceIdType.MESH
BLOCK = 16
F32 = jnp.float32
BF16 = jnp.bfloat16


def split_table(table):
    high = table.astype(ml_dtypes.bfloat16)
    low = (table - high.astype(np.float64)).astype(ml_dtypes.bfloat16)
    return high, low


def column_table(columns):
    phases = np.outer(np.arange(columns), np.arange(columns // 2)) % columns
    phases = 2.0 * math.pi / columns * phases
    return np.concatenate([np.cos(phases), -np.sin(phases)], axis=1) / math.sqrt(columns)


def row_table(height, rows_dev):
    table = np.zeros((2 * height, height // rows_dev * BLOCK))
    ids = np.arange(height)
    for device in range(height // rows_dev):
        for entry in range(rows_dev + 2):
            row = device * rows_dev + rows_dev - entry
            if 0 <= row < height:
                phase = 2.0 * math.pi / height * (ids * row % height)
                table[:height, device * BLOCK + entry] = np.cos(phase)
                table[height:, device * BLOCK + entry] = -np.sin(phase)
    return table / math.sqrt(height)


def halves(x):
    high = x.astype(BF16)
    return high, (x - high.astype(F32)).astype(BF16)


def dot(a, b, dims=((1,), (0,))):
    return lax.dot_general(a, b, (dims, ((), ())), preferred_element_type=F32)


def dot3(a, b, dims=((1,), (0,))):
    return dot(a[0], b[0], dims) + (dot(a[0], b[1], dims) + dot(a[1], b[0], dims))


def shift(x, by):
    columns = x.shape[-1]
    lane = lax.broadcasted_iota(jnp.int32, x.shape, 1)
    if by > 0:
        return jnp.where(lane < by, 0.0, pltpu.roll(x, by, 1))
    return jnp.where(lane >= columns + by, 0.0, pltpu.roll(x, columns + by, 1))


def main_kernel(
    sizes,
    features,
    weight,
    target,
    row_tables,
    col_tables,
    grad_features,
    grad_weight,
    loss_out,
    held,
    weight_in,
    target_in,
    row_held,
    col_held,
    acc,
    weight_acc,
    part,
    arrived,
    grad_send,
    grad_all,
    shifted,
    kernel_acc,
    terms,
    terms_in,
    terms_sum,
    load_sem,
    send_sem,
    recv_sem,
    back_send,
    back_recv,
    terms_send,
    terms_recv,
    sum_send,
    sum_recv,
):
    n_clip, n_row, n_ch, chunk, n_own = sizes
    frames_in, rows_dev, columns, channels = held.shape
    frames_out = frames_in - 2
    planes = 3 * frames_out
    n_group = n_row * n_ch
    n_all = n_clip * n_row
    clip, row, ch = (lax.axis_index(a) for a in ("clip", "row", "ch"))
    me = row * n_ch + ch
    rank = clip * n_row + row
    entries = float(planes * n_row * rows_dev * (columns // 2))

    loads = [
        pltpu.make_async_copy(features.at[0, f], held.at[f], load_sem.at[f])
        for f in range(frames_in)
    ]
    small = ((weight, weight_in), (target, target_in), (row_tables, row_held), (col_tables, col_held))
    for at, (source, place) in enumerate(small):
        loads.append(pltpu.make_async_copy(source, place, load_sem.at[frames_in + at]))
    for load in loads[frames_in : frames_in + 2] + loads[:frames_in] + loads[frames_in + 2 :]:
        load.start()

    barrier = pltpu.get_barrier_semaphore()

    @pl.loop(1, n_group)
    def _(p):
        other = lax.rem(me + p, n_group)
        pl.semaphore_signal(
            barrier,
            inc=1,
            device_id={"row": other // n_ch, "ch": lax.rem(other, n_ch)},
            device_id_type=MESH,
        )

    @pl.loop(n_row, n_all)
    def _(p):
        other = lax.rem(clip * n_row + p, n_all)
        pl.semaphore_signal(
            barrier,
            inc=1,
            device_id={"clip": other // n_row, "row": lax.rem(other, n_row)},
            device_id_type=MESH,
        )

    weight_acc[...] = jnp.zeros_like(weight_acc)
    acc[...] = jnp.zeros_like(acc)
    loads[frames_in].wait()
    loads[frames_in + 1].wait()
    for dt in range(3):
        for di in range(3):
            for dj in range(3):
                at = (dt * 3 + di) * BLOCK + dj * 3
                weight_acc[at : at + 3, :] = weight_in[dt, di, dj].astype(F32)
    taps = weight_acc[...].astype(BF16)

    @pl.when(ch == 0)
    def _():
        for t in range(frames_out):
            for o in range(3):
                frame = -target_in[0, o, t].astype(F32)
                for i in range(rows_dev):
                    acc[t, rows_dev - i, 3 + o, :] = frame[i]

    def exchange(t):
        for o in range(3):
            views = [acc[t, :, dj * 3 + o, :] for dj in range(3)]
            part[t * 3 + o] = views[1] + shift(views[0], 1) + shift(views[2], -1)
            plane = t * 3 + o

            @pl.when(me == plane)
            def _():
                arrived[plane] = part[plane]

            @pl.when(me != plane)
            def _():
                pltpu.make_async_remote_copy(
                    src_ref=part.at[plane],
                    dst_ref=arrived.at[me],
                    send_sem=send_sem.at[plane],
                    recv_sem=recv_sem.at[me],
                    device_id={"row": plane // n_ch, "ch": plane % n_ch},
                    device_id_type=MESH,
                ).start()

    for f in range(frames_in):
        loads[f].wait()
        low, top = max(0, f - frames_out + 1), min(2, f)
        chosen = taps[low * 3 * BLOCK : (top + 1) * 3 * BLOCK]

        @pl.loop(0, rows_dev, unroll=True)
        def _(r):
            made = dot(chosen, held[f, r], ((1,), (1,))).reshape(-1, BLOCK, columns)
            for dt in range(low, top + 1):
                at = (dt - low) * 3
                acc[f - dt, pl.ds(rows_dev - 1 - r, 3)] += made[at : at + 3]

        if f == 2:
            pl.semaphore_wait(barrier, n_group - 1 + n_all - n_row)
        if f >= 2:
            exchange(f - 2)

    loads[frames_in + 2].wait()
    loads[frames_in + 3].wait()

    @pl.when(me < planes)
    def _():
        @pl.loop(0, n_group)
        def _(s):
            @pl.when(s != me)
            def _():
                pltpu.make_async_copy(
                    arrived.at[s], arrived.at[s], recv_sem.at[s]
                ).wait()

        blocks = []
        for r in range(n_row):
            total = arrived[r * n_ch]
            for c in range(1, n_ch):
                total = total + arrived[r * n_ch + c]
            blocks.append(total)
        residual = jnp.concatenate(blocks, axis=0)
        height = n_row * rows_dev
        half = columns // 2
        basis = (col_held[0], col_held[1])
        rows_done = dot3((row_held[0], row_held[1]), halves(residual))
        both = dot3(halves(rows_done), basis)
        real = both[:height, :half] - both[height:, half:]
        imag = both[height:, :half] + both[:height, half:]
        power = real * real + imag * imag
        peak = jnp.max(power, keepdims=True)
        focal = power / (peak + 1e-05)
        loss = jnp.sum(focal * power, keepdims=True) / entries
        up_real = 2.0 * focal * real
        up_imag = 2.0 * focal * imag
        upstream = jnp.concatenate(
            [
                jnp.concatenate([up_real, up_imag], axis=1),
                jnp.concatenate([up_imag, -up_real], axis=1),
            ],
            axis=0,
        )
        columns_done = dot3(halves(upstream), basis, ((1,), (1,)))
        grads = dot3((row_held[2], row_held[3]), halves(columns_done))
        loss_high = loss.astype(BF16).astype(F32)
        loss_mid = (loss - loss_high).astype(BF16).astype(F32)
        loss_low = loss - loss_high - loss_mid
        entry = lax.rem(lax.broadcasted_iota(jnp.int32, grads.shape, 0), BLOCK)
        grads = jnp.where(entry == rows_dev + 2, loss_high, grads)
        grads = jnp.where(entry == rows_dev + 3, loss_mid, grads)
        grads = jnp.where(entry == rows_dev + 4, loss_low, grads)
        grads = grads.astype(BF16)
        for r in range(n_row):
            grad_send[r] = grads[r * BLOCK : (r + 1) * BLOCK]

        @pl.loop(1, n_group)
        def _(p):
            other = lax.rem(me + p, n_group)
            pltpu.make_async_remote_copy(
                src_ref=grad_send.at[other // n_ch],
                dst_ref=grad_all.at[me],
                send_sem=back_send.at[p],
                recv_sem=back_recv.at[me],
                device_id={"row": other // n_ch, "ch": lax.rem(other, n_ch)},
                device_id_type=MESH,
            ).start()

        grad_all[me] = grad_send[row]

    acc[...] = jnp.zeros_like(acc)
    for plane in range(planes):
        @pl.when(me != plane)
        def _():
            pltpu.make_async_copy(
                grad_all.at[plane], grad_all.at[plane], back_recv.at[plane]
            ).wait()

    loss_total = jnp.zeros((1, 128), F32)
    for plane in range(planes):
        t, o = divmod(plane, 3)
        grads = grad_all[plane].astype(F32)
        for part_at in range(3):
            at = rows_dev + 2 + part_at
            loss_total = loss_total + grads[at : at + 1, :128]
        entry = lax.broadcasted_iota(jnp.int32, grads.shape, 0)
        grads = jnp.where(entry < rows_dev + 2, grads, 0.0)
        for dj in range(3):
            moved = grads if dj == 1 else shift(grads, dj - 1)
            acc[t, :, dj * 3 + o, :] = moved
    loss_out[...] = loss_total
    for t in range(frames_out):
        shifted[t] = acc[t].reshape(BLOCK * BLOCK, columns).astype(BF16)

    kernel_acc[...] = jnp.zeros_like(kernel_acc)

    for f in range(frames_in):
        low, top = max(0, f - frames_out + 1), min(2, f)
        total = 0.0
        for r in range(rows_dev):
            begin = (rows_dev - 1 - r) * BLOCK
            stack = jnp.concatenate(
                [shifted[f - dt, begin : begin + 3 * BLOCK, :] for dt in range(low, top + 1)],
                axis=0,
            )
            total = total + dot(stack, held[f, r])
        kernel_acc[low * 3 * BLOCK : (top + 1) * 3 * BLOCK, :] += total

    terms[...] = jnp.zeros_like(terms)
    for b in range(9):
        terms[b * 9 : b * 9 + 9, :] = kernel_acc[b * BLOCK : b * BLOCK + 9, :]

    for m in range(n_own):
        @pl.when(rank == m)
        def _():
            terms_in[m] = terms[m * chunk : (m + 1) * chunk, :]

        @pl.when(rank != m)
        def _():
            pltpu.make_async_remote_copy(
                src_ref=terms.at[pl.ds(m * chunk, chunk)],
                dst_ref=terms_in.at[rank],
                send_sem=terms_send.at[m],
                recv_sem=terms_recv.at[rank],
                device_id={"clip": m // n_row, "row": m % n_row},
                device_id_type=MESH,
            ).start()

    def pull(f):
        low, top = max(0, f - frames_out + 1), min(2, f)
        chosen = taps[low * 3 * BLOCK : (top + 1) * 3 * BLOCK]
        for r in range(rows_dev):
            begin = (rows_dev - 1 - r) * BLOCK
            stack = jnp.concatenate(
                [shifted[f - dt, begin : begin + 3 * BLOCK, :] for dt in range(low, top + 1)],
                axis=0,
            )
            grad_features[0, f, r] = dot(stack, chosen, ((0,), (0,))).astype(BF16)

    for f in range(frames_in // 2):
        pull(f)

    @pl.when(rank < n_own)
    def _():
        @pl.loop(0, n_all)
        def _(s):
            @pl.when(s != rank)
            def _():
                pltpu.make_async_copy(
                    terms_in.at[s], terms_in.at[s], terms_recv.at[s]
                ).wait()

        terms_sum[rank] = jnp.sum(terms_in[...], axis=0)

        @pl.loop(1, n_all)
        def _(p):
            other = lax.rem(rank + p, n_all)
            pltpu.make_async_remote_copy(
                src_ref=terms_sum.at[rank],
                dst_ref=terms_sum.at[rank],
                send_sem=sum_send.at[p],
                recv_sem=sum_recv.at[rank],
                device_id={"clip": other // n_row, "row": lax.rem(other, n_row)},
                device_id_type=MESH,
            ).start()

    for f in range(frames_in // 2, frames_in):
        pull(f)

    for m in range(n_own):
        @pl.when(rank != m)
        def _():
            pltpu.make_async_copy(
                terms_sum.at[m], terms_sum.at[m], sum_recv.at[m]
            ).wait()

    for k in range(27):
        dt, di, dj = k // 9, k // 3 % 3, k % 3
        for o in range(3):
            m, at = divmod(k * 3 + o, chunk)
            grad_weight[dt, di, dj, o : o + 1, :] = terms_sum[m, at : at + 1, :]

    for plane in range(planes):
        @pl.when(me != plane)
        def _():
            pltpu.make_async_copy(part.at[plane], part.at[plane], send_sem.at[plane]).wait()

    @pl.when(me < planes)
    def _():
        @pl.loop(1, n_group)
        def _(p):
            pltpu.make_async_copy(grad_send.at[0], grad_send.at[0], back_send.at[p]).wait()

    for m in range(n_own):
        @pl.when(rank != m)
        def _():
            piece = terms.at[pl.ds(m * chunk, chunk)]
            pltpu.make_async_copy(piece, piece, terms_send.at[m]).wait()

    @pl.when(rank < n_own)
    def _():
        @pl.loop(1, n_all)
        def _(p):
            pltpu.make_async_copy(
                terms_sum.at[rank], terms_sum.at[rank], sum_send.at[p]
            ).wait()


def shards(features, weight, target):
    _, frames_in, rows_dev, columns, channels = features.shape
    frames_out = frames_in - 2
    planes = 3 * frames_out
    n_clip, n_row, n_ch = (lax.axis_size(a) for a in ("clip", "row", "ch"))
    n_group, n_all = n_row * n_ch, n_clip * n_row
    assert planes <= n_group and rows_dev + 5 <= BLOCK
    height = n_row * rows_dev
    pieces = -(-81 // 8)
    chunk = 8 * -(-pieces // n_all)
    n_own = -(-81 // chunk)
    rows = row_table(height, rows_dev)
    assert BLOCK == 2 * rows_dev
    row_tables = np.stack(split_table(rows) + split_table(rows.T))
    col_tables = np.stack(split_table(column_table(columns)))
    vmem = pl.BlockSpec(memory_space=pltpu.VMEM)
    inputs = tuple(
        pltpu.with_memory_space_constraint(x, pltpu.HBM)
        for x in (features, weight, target, jnp.asarray(row_tables), jnp.asarray(col_tables))
    )
    hbm = pl.BlockSpec(memory_space=pltpu.HBM)
    dma = pltpu.SemaphoreType.DMA
    grad_features, grad_weight, loss = pl.pallas_call(
        functools.partial(main_kernel, (n_clip, n_row, n_ch, chunk, n_own)),
        out_shape=(
            jax.ShapeDtypeStruct(features.shape, BF16),
            jax.ShapeDtypeStruct((3, 3, 3, 3, channels), F32),
            jax.ShapeDtypeStruct((1, 128), F32),
        ),
        in_specs=[hbm] * 5,
        out_specs=(vmem,) * 3,
        scratch_shapes=[
            pltpu.VMEM((frames_in, rows_dev, columns, channels), BF16),
            pltpu.VMEM(weight.shape, BF16),
            pltpu.VMEM(target.shape, BF16),
            pltpu.VMEM(row_tables.shape, BF16),
            pltpu.VMEM(col_tables.shape, BF16),
            pltpu.VMEM((frames_out, BLOCK, BLOCK, columns), F32),
            pltpu.VMEM((9 * BLOCK, channels), F32),
            pltpu.VMEM((planes, BLOCK, columns), F32),
            pltpu.VMEM((n_group, BLOCK, columns), F32),
            pltpu.VMEM((n_row, BLOCK, columns), BF16),
            pltpu.VMEM((planes, BLOCK, columns), BF16),
            pltpu.VMEM((frames_out, BLOCK * BLOCK, columns), BF16),
            pltpu.VMEM((9 * BLOCK, channels), F32),
            pltpu.VMEM((n_own * chunk, channels), F32),
            pltpu.VMEM((n_all, chunk, channels), F32),
            pltpu.VMEM((n_own, chunk, channels), F32),
            dma((frames_in + 4,)),
            dma((planes,)),
            dma((n_group,)),
            dma((n_group,)),
            dma((planes,)),
            dma((n_own,)),
            dma((n_all,)),
            dma((n_all,)),
            dma((n_own,)),
        ],
        compiler_params=pltpu.CompilerParams(
            collective_id=0, has_side_effects=True, vmem_limit_bytes=48 * 1024 * 1024
        ),
        name="main",
    )(*inputs)
    return (grad_features, grad_weight, loss[0, :1])


def solution(mesh):
    placed = (
        P("clip", None, "row", None, "ch"),
        P(None, None, None, None, "ch"),
        P("clip", None, None, "row", None),
    )
    return jax.shard_map(
        shards,
        mesh=mesh,
        in_specs=placed,
        out_specs=(P("clip", None, "row", None, "ch"), P(None, None, None, None, "ch"), P("clip")),
        check_vma=False,
    )
```

```python
import functools
import math

import jax
import jax.numpy as jnp
import ml_dtypes
import numpy as np
from jax import lax
from jax.experimental import pallas as pl
from jax.experimental.pallas import tpu as pltpu
from jax.sharding import PartitionSpec as P

MESH = pl.DeviceIdType.MESH
BLOCK = 16
F32 = jnp.float32
BF16 = jnp.bfloat16


def split_table(table):
    high = table.astype(ml_dtypes.bfloat16)
    low = (table - high.astype(np.float64)).astype(ml_dtypes.bfloat16)
    return high, low


def column_table(columns):
    phases = np.outer(np.arange(columns), np.arange(columns // 2)) % columns
    phases = 2.0 * math.pi / columns * phases
    return np.concatenate([np.cos(phases), -np.sin(phases)], axis=1) / math.sqrt(columns)


def row_table(height, rows_dev):
    table = np.zeros((2 * height, height // rows_dev * BLOCK))
    ids = np.arange(height)
    for device in range(height // rows_dev):
        for entry in range(rows_dev + 2):
            row = device * rows_dev + rows_dev - entry
            if 0 <= row < height:
                phase = 2.0 * math.pi / height * (ids * row % height)
                table[:height, device * BLOCK + entry] = np.cos(phase)
                table[height:, device * BLOCK + entry] = -np.sin(phase)
    return table / math.sqrt(height)


def halves(x):
    high = x.astype(BF16)
    return high, (x - high.astype(F32)).astype(BF16)


def dot(a, b, dims=((1,), (0,))):
    return lax.dot_general(a, b, (dims, ((), ())), preferred_element_type=F32)


def dot3(a, b, dims=((1,), (0,))):
    count = a[0].shape[0]
    both = dot(jnp.concatenate(a, axis=0), b[0], dims)
    return both[:count] + (both[count:] + dot(a[0], b[1], dims))


def swap_table(rows, columns):
    left = lax.broadcasted_iota(jnp.int32, (rows, columns), 0)
    right = lax.broadcasted_iota(jnp.int32, (rows, columns), 1)
    match = (left // BLOCK == right % BLOCK) & (left % BLOCK == right // BLOCK)
    return match.astype(F32).astype(BF16)


def plane_owners(planes, n_row, n_ch):
    if planes == 6 and n_row % 4 == 0 and n_ch == 2:
        places = ((0, 0), (3, 1), (0, 1), (1, 0), (2, 1), (2, 0))
        return [(row * (n_row // 4), ch) for row, ch in places]
    return [(plane // n_ch, plane % n_ch) for plane in range(planes)]


def shift(x, by):
    columns = x.shape[-1]
    lane = lax.broadcasted_iota(jnp.int32, x.shape, 1)
    if by > 0:
        return jnp.where(lane < by, 0.0, pltpu.roll(x, by, 1))
    return jnp.where(lane >= columns + by, 0.0, pltpu.roll(x, columns + by, 1))


def main_kernel(
    sizes,
    features,
    weight,
    target,
    row_tables,
    col_tables,
    grad_features,
    grad_weight,
    loss_out,
    held,
    weight_in,
    target_in,
    row_held,
    col_held,
    acc,
    weight_acc,
    part,
    arrived,
    grad_send,
    grad_all,
    shifted,
    kernel_acc,
    terms,
    terms_in,
    terms_sum,
    load_sem,
    send_sem,
    recv_sem,
    back_send,
    back_recv,
    terms_send,
    terms_recv,
    sum_send,
    sum_recv,
):
    n_clip, n_row, n_ch, chunk, n_own = sizes
    frames_in, rows_dev, columns, channels = held.shape
    frames_out = frames_in - 2
    planes = 3 * frames_out
    n_group = n_row * n_ch
    n_all = n_clip * n_row
    clip, row, ch = (lax.axis_index(a) for a in ("clip", "row", "ch"))
    me = row * n_ch + ch
    owners = plane_owners(planes, n_row, n_ch)
    slots = [at_row * n_ch + at_ch for at_row, at_ch in owners]
    owning = me == slots[0]
    for slot in slots[1:]:
        owning = owning | (me == slot)
    lines = (rows_dev + 2) * BLOCK
    rank = clip * n_row + row
    entries = float(planes * n_row * rows_dev * (columns // 2))

    loads = [
        pltpu.make_async_copy(features.at[0, f], held.at[f], load_sem.at[f])
        for f in range(frames_in)
    ]
    small = ((weight, weight_in), (target, target_in), (row_tables, row_held), (col_tables, col_held))
    for at, (source, place) in enumerate(small):
        loads.append(pltpu.make_async_copy(source, place, load_sem.at[frames_in + at]))
    for load in loads[frames_in : frames_in + 2] + loads[:frames_in] + loads[frames_in + 2 :]:
        load.start()

    barrier = pltpu.get_barrier_semaphore()

    @pl.loop(1, n_group)
    def _(p):
        other = lax.rem(me + p, n_group)
        pl.semaphore_signal(
            barrier,
            inc=1,
            device_id={"row": other // n_ch, "ch": lax.rem(other, n_ch)},
            device_id_type=MESH,
        )

    @pl.loop(n_row, n_all)
    def _(p):
        other = lax.rem(clip * n_row + p, n_all)
        pl.semaphore_signal(
            barrier,
            inc=1,
            device_id={"clip": other // n_row, "row": lax.rem(other, n_row)},
            device_id_type=MESH,
        )

    weight_acc[...] = jnp.zeros_like(weight_acc)
    acc[...] = jnp.zeros_like(acc)
    loads[frames_in].wait()
    loads[frames_in + 1].wait()
    for dt in range(3):
        for di in range(3):
            for dj in range(3):
                at = (dt * 3 + di) * BLOCK + dj * 3
                weight_acc[at : at + 3, :] = weight_in[dt, di, dj].astype(F32)
    taps = weight_acc[...].astype(BF16)

    @pl.when(ch == 0)
    def _():
        for t in range(frames_out):
            for o in range(3):
                frame = -target_in[0, o, t].astype(F32)
                for i in range(rows_dev):
                    acc[t, (rows_dev - i) * BLOCK + 3 + o, :] = frame[i]

    swap = swap_table(9 * BLOCK, lines)
    swap_back = swap_table(lines, 9 * BLOCK)

    def exchange(t):
        high, low = halves(acc[t])
        swapped = dot(swap, high) + dot(swap, low)
        third = 3 * BLOCK
        frame = (
            swapped[third : 2 * third]
            + shift(swapped[:third], 1)
            + shift(swapped[2 * third :], -1)
        )
        for o in range(3):
            plane = t * 3 + o
            part[plane] = frame[o * BLOCK : (o + 1) * BLOCK]

            @pl.when(me == slots[plane])
            def _():
                arrived[slots[plane]] = part[plane]

            @pl.when(me != slots[plane])
            def _():
                pltpu.make_async_remote_copy(
                    src_ref=part.at[plane],
                    dst_ref=arrived.at[me],
                    send_sem=send_sem.at[plane],
                    recv_sem=recv_sem.at[me],
                    device_id={"row": owners[plane][0], "ch": owners[plane][1]},
                    device_id_type=MESH,
                ).start()

    for f in range(frames_in):
        loads[f].wait()
        low, top = max(0, f - frames_out + 1), min(2, f)
        chosen = taps[low * 3 * BLOCK : (top + 1) * 3 * BLOCK]

        @pl.loop(0, rows_dev, unroll=True)
        def _(r):
            made = dot(chosen, held[f, r], ((1,), (1,)))
            begin = pl.multiple_of((rows_dev - 1 - r) * BLOCK, BLOCK)
            for dt in range(low, top + 1):
                at = (dt - low) * 3 * BLOCK
                acc[f - dt, pl.ds(begin, 3 * BLOCK), :] += made[at : at + 3 * BLOCK]

        if f == 2:
            pl.semaphore_wait(barrier, n_group - 1 + n_all - n_row)
        if f >= 2:
            exchange(f - 2)

    loads[frames_in + 2].wait()
    loads[frames_in + 3].wait()

    @pl.when(owning)
    def _():
        @pl.loop(0, n_group)
        def _(s):
            @pl.when(s != me)
            def _():
                piece = arrived.at[s]
                pltpu.make_async_copy(piece, piece, recv_sem.at[s]).wait()

        blocks = []
        for r in range(n_row):
            total = arrived[r * n_ch]
            for c in range(1, n_ch):
                total = total + arrived[r * n_ch + c]
            blocks.append(total)
        residual = jnp.concatenate(blocks, axis=0)
        height = n_row * rows_dev
        half = columns // 2
        basis = (col_held[0], col_held[1])
        rows_done = dot3((row_held[0], row_held[1]), halves(residual))
        both = dot3(halves(rows_done), basis)
        real = both[:height, :half] - both[height:, half:]
        imag = both[height:, :half] + both[:height, half:]
        power = real * real + imag * imag
        peak = jnp.max(power, keepdims=True)
        focal = power / (peak + 1e-05)
        loss = jnp.sum(focal * power, keepdims=True) / entries
        up_real = 2.0 * focal * real
        up_imag = 2.0 * focal * imag
        upstream = jnp.concatenate(
            [
                jnp.concatenate([up_real, up_imag], axis=1),
                jnp.concatenate([up_imag, -up_real], axis=1),
            ],
            axis=0,
        )
        columns_done = dot3(halves(upstream), basis, ((1,), (1,)))
        grads = dot3((row_held[2], row_held[3]), halves(columns_done))
        loss_high = loss.astype(BF16).astype(F32)
        loss_mid = (loss - loss_high).astype(BF16).astype(F32)
        loss_low = loss - loss_high - loss_mid
        entry = lax.rem(lax.broadcasted_iota(jnp.int32, grads.shape, 0), BLOCK)
        grads = jnp.where(entry == rows_dev + 2, loss_high, grads)
        grads = jnp.where(entry == rows_dev + 3, loss_mid, grads)
        grads = jnp.where(entry == rows_dev + 4, loss_low, grads)
        grads = grads.astype(BF16)
        for r in range(n_row):
            grad_send[r] = grads[r * BLOCK : (r + 1) * BLOCK]

        @pl.loop(1, n_group)
        def _(p):
            other = lax.rem(me + p, n_group)
            pltpu.make_async_remote_copy(
                src_ref=grad_send.at[other // n_ch],
                dst_ref=grad_all.at[me],
                send_sem=back_send.at[p],
                recv_sem=back_recv.at[me],
                device_id={"row": other // n_ch, "ch": lax.rem(other, n_ch)},
                device_id_type=MESH,
            ).start()

        grad_all[me] = grad_send[row]

    loss_total = jnp.zeros((1, 128), F32)
    for t in range(frames_out):
        for slot in slots[3 * t : 3 * t + 3]:
            @pl.when(me != slot)
            def _():
                pltpu.make_async_copy(
                    grad_all.at[slot], grad_all.at[slot], back_recv.at[slot]
                ).wait()

        frame = jnp.concatenate([grad_all[slot] for slot in slots[3 * t : 3 * t + 3]], axis=0)
        frame = frame.astype(F32)
        for o in range(3):
            for at in range(rows_dev + 2, rows_dev + 5):
                loss_total = loss_total + frame[o * BLOCK + at : o * BLOCK + at + 1, :128]
        moved = jnp.concatenate([shift(frame, -1), frame, shift(frame, 1)], axis=0)
        shifted[t] = dot(swap_back, moved.astype(BF16)).astype(BF16)
    loss_out[...] = loss_total

    kernel_acc[...] = jnp.zeros_like(kernel_acc)

    for f in range(frames_in):
        low, top = max(0, f - frames_out + 1), min(2, f)
        total = 0.0
        for r in range(rows_dev):
            begin = (rows_dev - 1 - r) * BLOCK
            stack = jnp.concatenate(
                [shifted[f - dt, begin : begin + 3 * BLOCK, :] for dt in range(low, top + 1)],
                axis=0,
            )
            total = total + dot(stack, held[f, r])
        kernel_acc[low * 3 * BLOCK : (top + 1) * 3 * BLOCK, :] += total

    terms[...] = jnp.zeros_like(terms)
    for b in range(9):
        terms[b * 9 : b * 9 + 9, :] = kernel_acc[b * BLOCK : b * BLOCK + 9, :]

    for m in range(n_own):
        @pl.when(rank == m)
        def _():
            terms_in[m] = terms[m * chunk : (m + 1) * chunk, :]

        @pl.when(rank != m)
        def _():
            pltpu.make_async_remote_copy(
                src_ref=terms.at[pl.ds(m * chunk, chunk)],
                dst_ref=terms_in.at[rank],
                send_sem=terms_send.at[m],
                recv_sem=terms_recv.at[rank],
                device_id={"clip": m // n_row, "row": m % n_row},
                device_id_type=MESH,
            ).start()

    def pull(f):
        low, top = max(0, f - frames_out + 1), min(2, f)
        chosen = taps[low * 3 * BLOCK : (top + 1) * 3 * BLOCK]
        for r in range(rows_dev):
            begin = (rows_dev - 1 - r) * BLOCK
            stack = jnp.concatenate(
                [shifted[f - dt, begin : begin + 3 * BLOCK, :] for dt in range(low, top + 1)],
                axis=0,
            )
            grad_features[0, f, r] = dot(stack, chosen, ((0,), (0,))).astype(BF16)

    for f in range(frames_in // 2):
        pull(f)

    @pl.when(rank < n_own)
    def _():
        @pl.loop(0, n_all)
        def _(s):
            @pl.when(s != rank)
            def _():
                pltpu.make_async_copy(
                    terms_in.at[s], terms_in.at[s], terms_recv.at[s]
                ).wait()

        terms_sum[rank] = jnp.sum(terms_in[...], axis=0)

        @pl.loop(1, n_all)
        def _(p):
            other = lax.rem(rank + p, n_all)
            pltpu.make_async_remote_copy(
                src_ref=terms_sum.at[rank],
                dst_ref=terms_sum.at[rank],
                send_sem=sum_send.at[p],
                recv_sem=sum_recv.at[rank],
                device_id={"clip": other // n_row, "row": lax.rem(other, n_row)},
                device_id_type=MESH,
            ).start()

    for f in range(frames_in // 2, frames_in):
        pull(f)

    for m in range(n_own):
        @pl.when(rank != m)
        def _():
            pltpu.make_async_copy(
                terms_sum.at[m], terms_sum.at[m], sum_recv.at[m]
            ).wait()

    for k in range(27):
        dt, di, dj = k // 9, k // 3 % 3, k % 3
        for o in range(3):
            m, at = divmod(k * 3 + o, chunk)
            grad_weight[dt, di, dj, o : o + 1, :] = terms_sum[m, at : at + 1, :]

    for plane in range(planes):
        @pl.when(me != slots[plane])
        def _():
            piece = part.at[plane]
            pltpu.make_async_copy(piece, piece, send_sem.at[plane]).wait()

    @pl.when(owning)
    def _():
        @pl.loop(1, n_group)
        def _(p):
            pltpu.make_async_copy(grad_send.at[0], grad_send.at[0], back_send.at[p]).wait()

    for m in range(n_own):
        @pl.when(rank != m)
        def _():
            piece = terms.at[pl.ds(m * chunk, chunk)]
            pltpu.make_async_copy(piece, piece, terms_send.at[m]).wait()

    @pl.when(rank < n_own)
    def _():
        @pl.loop(1, n_all)
        def _(p):
            pltpu.make_async_copy(
                terms_sum.at[rank], terms_sum.at[rank], sum_send.at[p]
            ).wait()


def shards(features, weight, target):
    _, frames_in, rows_dev, columns, channels = features.shape
    frames_out = frames_in - 2
    planes = 3 * frames_out
    n_clip, n_row, n_ch = (lax.axis_size(a) for a in ("clip", "row", "ch"))
    n_group, n_all = n_row * n_ch, n_clip * n_row
    assert planes <= n_group and rows_dev + 5 <= BLOCK
    height = n_row * rows_dev
    pieces = -(-81 // 8)
    chunk = 8 * -(-pieces // n_all)
    n_own = -(-81 // chunk)
    rows = row_table(height, rows_dev)
    assert BLOCK == 2 * rows_dev
    row_tables = np.stack(split_table(rows) + split_table(rows.T))
    col_tables = np.stack(split_table(column_table(columns)))
    vmem = pl.BlockSpec(memory_space=pltpu.VMEM)
    inputs = tuple(
        pltpu.with_memory_space_constraint(x, pltpu.HBM)
        for x in (features, weight, target, jnp.asarray(row_tables), jnp.asarray(col_tables))
    )
    hbm = pl.BlockSpec(memory_space=pltpu.HBM)
    dma = pltpu.SemaphoreType.DMA
    grad_features, grad_weight, loss = pl.pallas_call(
        functools.partial(main_kernel, (n_clip, n_row, n_ch, chunk, n_own)),
        out_shape=(
            jax.ShapeDtypeStruct(features.shape, BF16),
            jax.ShapeDtypeStruct((3, 3, 3, 3, channels), F32),
            jax.ShapeDtypeStruct((1, 128), F32),
        ),
        in_specs=[hbm] * 5,
        out_specs=(vmem,) * 3,
        scratch_shapes=[
            pltpu.VMEM((frames_in, rows_dev, columns, channels), BF16),
            pltpu.VMEM(weight.shape, BF16),
            pltpu.VMEM(target.shape, BF16),
            pltpu.VMEM(row_tables.shape, BF16),
            pltpu.VMEM(col_tables.shape, BF16),
            pltpu.VMEM((frames_out, (rows_dev + 2) * BLOCK, columns), F32),
            pltpu.VMEM((9 * BLOCK, channels), F32),
            pltpu.VMEM((planes, BLOCK, columns), F32),
            pltpu.VMEM((n_group, BLOCK, columns), F32),
            pltpu.VMEM((n_row, BLOCK, columns), BF16),
            pltpu.VMEM((n_group, BLOCK, columns), BF16),
            pltpu.VMEM((frames_out, (rows_dev + 2) * BLOCK, columns), BF16),
            pltpu.VMEM((9 * BLOCK, channels), F32),
            pltpu.VMEM((n_own * chunk, channels), F32),
            pltpu.VMEM((n_all, chunk, channels), F32),
            pltpu.VMEM((n_own, chunk, channels), F32),
            dma((frames_in + 4,)),
            dma((planes,)),
            dma((n_group,)),
            dma((n_group,)),
            dma((n_group,)),
            dma((n_own,)),
            dma((n_all,)),
            dma((n_all,)),
            dma((n_own,)),
        ],
        compiler_params=pltpu.CompilerParams(
            collective_id=0, has_side_effects=True, vmem_limit_bytes=48 * 1024 * 1024
        ),
        name="main",
    )(*inputs)
    return (grad_features, grad_weight, loss[0, :1])


def solution(mesh):
    placed = (
        P("clip", None, "row", None, "ch"),
        P(None, None, None, None, "ch"),
        P("clip", None, None, "row", None),
    )
    return jax.shard_map(
        shards,
        mesh=mesh,
        in_specs=placed,
        out_specs=(P("clip", None, "row", None, "ch"), P(None, None, None, None, "ch"), P("clip")),
        check_vma=False,
    )
```
